32 devices in a mesh: gx: 4 (over y, x), gy: 2 (over core), gz: 4 (over z).
Axes of the slice: x: 2, y: 2, z: 4, core: 2. Of those that a mesh axis runs over, the one named last changes fastest.
Arguments:
- flexibility: bfloat16 [4, 2, 4, 768, 768], P('gx', 'gy', 'gz'), may hold values from -6 to 6, as said below
- stiffness: bfloat16 [4, 2, 4, 768, 768], P('gx', 'gy', 'gz'), may hold values from -6 to 6, as said below
- local_load: float32 [4, 2, 4, 6, 128, 128], P('gx', 'gy', 'gz'), may hold values from -80 to 80
- face_map: int32 [4, 2, 4, 6, 128], P('gx', 'gy', 'gz'), may hold values from 0 to 127, each once within a row
- face_sign: int32 [4, 2, 4, 6, 128], P('gx', 'gy', 'gz'), may hold values from -1 to 1, as said below
Outputs:
- multipliers: float32 [4, 2, 4, 3, 128, 128], P('gx', 'gy', 'gz')
- residual: float32 [4, 2, 4, 3, 128, 128], P('gx', 'gy', 'gz')
The draws below stay inside these ranges and needn't reach their ends.
Inputs may be any that keep to these rules, and one draw needn't show every extreme that they name: `face_map`: each row is a permutation of 0 to 127. `face_sign`: every entry is +1 or -1, and the two subdomains sharing a face give each of its multipliers opposite signs. `flexibility`: each subdomain's matrix is symmetric positive definite. `stiffness`: each subdomain's matrix is symmetric positive definite.
All inputs are finite; a program needn't handle non-finite values.
Results may differ from the reference program's by a relative error of at most 0.011.
Values sent between devices are 32-bit elements; how exact they have to be, the bound alone decides.
A program may use at most 64 MiB of HBM per device.

```python
import math
import jax
import jax.numpy as jnp
from jax import lax

FACE = 128
RESP = 128
ITERS = 2
SUB_X = 4
SUB_Y = 2
SUB_Z = 4


def operator_draw(key, scale_low, scale_high):
    order = 6 * FACE
    shape = (SUB_X, SUB_Y, SUB_Z, order, order)
    noise = jnp.clip(jax.random.normal(jax.random.fold_in(key, 1), shape, jnp.float32), -5.0, 5.0)
    coupling = (noise + jnp.swapaxes(noise, -1, -2)) * (0.42 / math.sqrt(2.0 * order))
    base = jnp.eye(order, dtype=jnp.float32) + coupling
    logs = jax.random.uniform(jax.random.fold_in(key, 2), shape[:-1], jnp.float32, math.log(scale_low), math.log(scale_high))
    roots = jnp.sqrt(jnp.exp(logs))
    return (roots[..., :, None] * base * roots[..., None, :]).astype(jnp.bfloat16)


def draw_flexibility(key, part):
    return operator_draw(jax.random.fold_in(key, 11), 0.5, 2.0)


def draw_stiffness(key, part):
    return operator_draw(jax.random.fold_in(key, 23), 0.5, 2.0)


def draw_face_sign(key, part):
    sign_bits = jax.random.randint(jax.random.fold_in(key, 5), (SUB_X, SUB_Y, SUB_Z, 3, FACE), 0, 2)
    lower_sign = 2 * sign_bits - 1
    stacked = []
    for dimension in range(3):
        lower_face = lower_sign[:, :, :, dimension]
        stacked.append(lower_face)
        stacked.append(-jnp.roll(lower_face, -1, axis=dimension))
    return jnp.stack(stacked, axis=3).astype(jnp.int32)


def draw_local_load(key, part):
    shape = (SUB_X, SUB_Y, SUB_Z, 6, FACE, RESP)
    pos_x = jnp.arange(SUB_X, dtype=jnp.float32) / max(SUB_X - 1, 1)
    pos_y = jnp.arange(SUB_Y, dtype=jnp.float32) / max(SUB_Y - 1, 1)
    pos_z = jnp.arange(SUB_Z, dtype=jnp.float32) / max(SUB_Z - 1, 1)
    rising = 3.0 ** ((pos_x[:, None, None] + pos_y[None, :, None] + pos_z[None, None, :]) / 3.0)
    column_scale = jnp.exp(jax.random.uniform(jax.random.fold_in(key, 3), (RESP,), jnp.float32, math.log(0.3), math.log(3.0)))
    base = jnp.clip(jax.random.normal(jax.random.fold_in(key, 4), shape, jnp.float32), -4.0, 4.0)
    amplitude = rising[:, :, :, None, None, None]
    return (base * amplitude * column_scale).astype(jnp.float32)


def setup_inputs(seed: int = 0) -> dict:
    keys = jax.random.split(jax.random.key(seed), 6)
    return {
        "flexibility": draw_flexibility(jax.random.fold_in(keys[5], 71), 0),
        "stiffness": draw_stiffness(jax.random.fold_in(keys[5], 71), 0),
        "local_load": draw_local_load(jax.random.fold_in(keys[5], 71), 0),
        "face_map": jax.vmap(lambda own: jax.random.permutation(own, FACE))(jax.random.split(keys[3], SUB_X * SUB_Y * SUB_Z * 6)).reshape((SUB_X, SUB_Y, SUB_Z, 6, FACE)).astype(jnp.int32),
        "face_sign": draw_face_sign(jax.random.fold_in(keys[5], 71), 0),
    }


def local_apply(operator, face_map, face_sign, vector):
    width = face_map.shape[-1]
    columns = vector.shape[-1]
    face_rows = (jnp.arange(6, dtype=jnp.int32)[:, None] * width + face_map).reshape(-1).astype(jnp.int32)
    signs = face_sign.astype(jnp.float32)[:, :, None]
    signed = (signs * vector).reshape(6 * width, columns)
    scattered = jnp.zeros((6 * width, columns), jnp.float32).at[face_rows].set(signed)
    product = jnp.dot(operator, scattered.astype(jnp.bfloat16), preferred_element_type=jnp.float32)
    gathered = product[face_rows].reshape(6, width, columns)
    return signs * gathered


def local_entry(packed):
    return local_apply(packed[0], packed[1], packed[2], packed[3])


def assemble(vector):
    assembled = []
    for dimension in range(3):
        lower_face = vector[:, :, :, 2 * dimension]
        upper_face = vector[:, :, :, 2 * dimension + 1]
        assembled.append(lower_face + jnp.roll(upper_face, 1, axis=dimension))
        assembled.append(upper_face + jnp.roll(lower_face, -1, axis=dimension))
    return jnp.stack(assembled, axis=3)


def apply_operator(operators, face_map, face_sign, vector):
    grid = vector.shape[:3]
    count = grid[0] * grid[1] * grid[2]
    order = operators.shape[-1]
    width = face_map.shape[-1]
    columns = vector.shape[-1]
    packed = (operators.reshape(count, order, order), face_map.reshape(count, 6, width),
              face_sign.reshape(count, 6, width), vector.reshape(count, 6, width, columns))
    locals_out = lax.map(local_entry, packed)
    return assemble(locals_out.reshape(vector.shape))


def inner(first, second):
    return jnp.sum(first[:, :, :, 0::2] * second[:, :, :, 0::2], axis=(0, 1, 2, 3, 4))


def reference(flexibility, stiffness, local_load, face_map, face_sign):
    residual = assemble(local_load)
    multipliers = jnp.zeros_like(residual)
    precond = apply_operator(stiffness, face_map, face_sign, residual)
    image_z = apply_operator(flexibility, face_map, face_sign, precond)
    gamma_now = inner(residual, precond)
    delta_now = inner(precond, image_z)
    step_size = gamma_now / delta_now
    direction = precond
    image_dir = image_z
    for iteration in range(ITERS):
        multipliers = multipliers + step_size * direction
        residual = residual - step_size * image_dir
        if iteration + 1 < ITERS:
            precond = apply_operator(stiffness, face_map, face_sign, residual)
            image_z = apply_operator(flexibility, face_map, face_sign, precond)
            gamma_new = inner(residual, precond)
            delta_now = inner(precond, image_z)
            conjugacy = gamma_new / gamma_now
            step_size = gamma_new / (delta_now - conjugacy * gamma_new / step_size)
            direction = precond + conjugacy * direction
            image_dir = image_z + conjugacy * image_dir
            gamma_now = gamma_new
    return multipliers[:, :, :, 0::2], residual[:, :, :, 0::2]
```

```python
import functools
import jax
import jax.numpy as jnp
from jax import lax
from jax.experimental import pallas as pl
from jax.experimental.pallas import tpu as pltpu
from jax.sharding import PartitionSpec as P

AXES = ("gx", "gy", "gz")
ARRIVAL = (1, 0, 2)
MESH = pl.DeviceIdType.MESH


def kernel(
    sizes, stiff_hbm, flex_hbm, load_hbm, map_ref, sign_ref, mult_ref, res_ref,
    raw, mid, ops, load, own, got, acc, vec, gat_x, gat_y, gat_z,
    local_sem, send_sem, recv_sem, sx, rx, sy, ry, sz, rz,
):
    width, columns = load.shape[1:]
    pair = 2 * width
    me = [lax.axis_index(axis) for axis in AXES]

    local = [
        pltpu.make_async_copy(load_hbm, load, local_sem.at[0]),
        pltpu.make_async_copy(stiff_hbm, raw.at[0], local_sem.at[1]),
        pltpu.make_async_copy(flex_hbm, raw.at[1], local_sem.at[2]),
    ]
    for copy in local:
        copy.start()

    barrier = pltpu.get_barrier_semaphore()
    for d, axis in enumerate(AXES):
        for k in range(1, sizes[d]):
            pl.semaphore_signal(
                barrier, inc=1, device_id={axis: lax.rem(me[d] + k, sizes[d])}, device_id_type=MESH
            )
    pl.semaphore_wait(barrier, sum(sizes) - 3)

    sent = []

    def send_face(exchange, face, source):
        d, upper = face // 2, face % 2
        step = 1 if upper else sizes[d] - 1
        there = face - 1 if upper else face + 1
        copy = pltpu.make_async_remote_copy(
            src_ref=source.at[face],
            dst_ref=got.at[exchange, there],
            send_sem=send_sem.at[exchange, face],
            recv_sem=recv_sem.at[exchange, there],
            device_id={AXES[d]: lax.rem(me[d] + step, sizes[d])},
            device_id_type=MESH,
        )
        copy.start()
        sent.append(copy)
        return copy

    gathers = ((gat_x, sx, rx), (gat_y, sy, ry), (gat_z, sz, rz))

    def gather_start(which, d, value):
        buf, ssem, rsem = gathers[d]
        buf[which, me[d]] = value
        for k in range(1, sizes[d]):
            peer = lax.rem(me[d] + k, sizes[d])
            copy = pltpu.make_async_remote_copy(
                src_ref=buf.at[which, me[d]],
                dst_ref=buf.at[which, me[d]],
                send_sem=ssem.at[which, k],
                recv_sem=rsem.at[which, me[d]],
                device_id={AXES[d]: peer},
                device_id_type=MESH,
            )
            copy.start()
            sent.append(copy)

    def gather_finish(which, d):
        buf, ssem, rsem = gathers[d]
        for k in range(1, sizes[d]):
            peer = lax.rem(me[d] + k, sizes[d])
            pltpu.make_async_remote_copy(
                src_ref=buf.at[which, peer],
                dst_ref=buf.at[which, peer],
                send_sem=ssem.at[which, k],
                recv_sem=rsem.at[which, peer],
                device_id={AXES[d]: peer},
                device_id_type=MESH,
            ).wait_recv()
        total = buf[which, 0]
        for k in range(1, sizes[d]):
            total = total + buf[which, k]
        return total

    def rows(d):
        return slice(d * pair, (d + 1) * pair)

    def flat(value):
        return value.reshape(pair, columns)

    def faces(ref, d):
        return flat(ref[2 * d : 2 * d + 2])

    def fold(which):
        for d in range(3):
            low = map_ref[2 * d : 2 * d + 1, :]
            high = map_ref[2 * d + 1 : 2 * d + 2, :] + width
            row = jnp.concatenate([low, high], axis=1)
            sign = jnp.concatenate(
                [sign_ref[2 * d : 2 * d + 1, :], sign_ref[2 * d + 1 : 2 * d + 2, :]], axis=1
            ).astype(jnp.float32)
            place = lax.broadcasted_iota(jnp.int32, (pair, pair), 0)
            pick = jnp.where(place == row, sign, 0.0)
            mid[:, rows(d)] = jnp.dot(
                raw[which, :, rows(d)], pick.astype(jnp.bfloat16), preferred_element_type=jnp.float32
            ).astype(jnp.bfloat16)
        for d in range(3):
            low = map_ref[2 * d : 2 * d + 1, :]
            high = map_ref[2 * d + 1 : 2 * d + 2, :] + width
            row = jnp.concatenate([low, high], axis=1)
            sign = jnp.concatenate(
                [sign_ref[2 * d : 2 * d + 1, :], sign_ref[2 * d + 1 : 2 * d + 2, :]], axis=1
            ).astype(jnp.float32)
            place = lax.broadcasted_iota(jnp.int32, (pair, pair), 0)
            pick = jnp.where(place == row, sign, 0.0).T
            ops[which, rows(d), :] = jnp.dot(
                pick.astype(jnp.bfloat16), mid[rows(d), :], preferred_element_type=jnp.float32
            ).astype(jnp.bfloat16)

    def product(block, value, split):
        high = value.astype(jnp.bfloat16)
        if not split:
            return jnp.dot(block, high, preferred_element_type=jnp.float32)
        low = (value - high.astype(jnp.float32)).astype(jnp.bfloat16)
        both = jnp.dot(block, jnp.concatenate([high, low], axis=1), preferred_element_type=jnp.float32)
        return both[:, :columns] + both[:, columns:]

    def apply(which, get, out, split, ready=None):
        first = product(ops[which, :, rows(ARRIVAL[0])], get(ARRIVAL[0]), split)
        acc[...] = first
        acc[...] += product(ops[which, :, rows(ARRIVAL[1])], get(ARRIVAL[1]), split)
        last = get(ARRIVAL[2])
        for d in reversed(ARRIVAL):
            value = acc[rows(d), :] + product(ops[which, rows(d), rows(ARRIVAL[2])], last, split)
            own[out, 2 * d : 2 * d + 2] = value.reshape(2, width, columns)
            if ready is not None:
                ready(d)

    def sender(exchange):
        def ready(d):
            waits[exchange, 2 * d + 1] = send_face(exchange, 2 * d, own.at[exchange - 1])
            waits[exchange, 2 * d] = send_face(exchange, 2 * d + 1, own.at[exchange - 1])

        return ready

    waits = {}

    def arrive(exchange, d):
        waits[exchange, 2 * d].wait_recv()
        waits[exchange, 2 * d + 1].wait_recv()
        return flat(got[exchange, 2 * d : 2 * d + 2])

    def inner(first, second):
        total = jnp.zeros((8, columns), jnp.float32)
        for d in range(3):
            term = faces(first, d) * faces(second, d)
            total = total + jnp.sum(term.reshape(pair // 8, 8, columns), axis=0)
        return total

    def down(value):
        return jnp.sum(value, axis=0, keepdims=True)

    r0, z0, w0, r1, z1 = (vec.at[k] for k in range(5))

    def keep(ref, d, value):
        ref[2 * d : 2 * d + 2] = value.reshape(2, width, columns)
        return value

    for d in reversed(ARRIVAL):
        waits[0, 2 * d + 1] = send_face(0, 2 * d, load_hbm)
        waits[0, 2 * d] = send_face(0, 2 * d + 1, load_hbm)
    local[1].wait()
    fold(0)
    local[0].wait()
    apply(0, lambda d: keep(r0, d, faces(load, d) + arrive(0, d)), 0, True, sender(1))
    gamma_part = inner(r0, own.at[0])
    local[2].wait()
    fold(1)

    apply(1, lambda d: keep(z0, d, faces(own.at[0], d) + arrive(1, d)), 1, False)
    gather_start(0, 1, jnp.stack([gamma_part, inner(z0, own.at[1])]))
    for d in reversed(ARRIVAL):
        sender(2)(d)
    gather_start(0, 0, gather_finish(0, 1))

    apply(0, lambda d: keep(w0, d, faces(own.at[1], d) + arrive(2, d)), 2, True, sender(3))
    gather_start(0, 2, gather_finish(0, 0))
    sums = gather_finish(0, 2)
    gamma0, delta0 = down(sums[0]), down(sums[1])
    alpha0 = gamma0 / delta0

    gamma_part = jnp.zeros((8, columns), jnp.float32)
    for d in range(3):
        value = keep(r1, d, faces(r0, d) - alpha0 * faces(w0, d))
        term = value * (faces(own.at[0], d) - alpha0 * faces(own.at[2], d))
        gamma_part = gamma_part + jnp.sum(term.reshape(pair // 8, 8, columns), axis=0)

    apply(
        1,
        lambda d: keep(z1, d, faces(z0, d) - alpha0 * (faces(own.at[2], d) + arrive(3, d))),
        3,
        False,
    )
    gather_start(1, 1, jnp.stack([gamma_part, inner(z1, own.at[3])]))
    for d in reversed(ARRIVAL):
        waits[4, 2 * d] = send_face(4, 2 * d + 1, own.at[3])
    gather_start(1, 0, gather_finish(1, 1))
    gather_start(1, 2, gather_finish(1, 0))
    sums = gather_finish(1, 2)
    gamma1, delta1 = down(sums[0]), down(sums[1])
    beta = gamma1 / gamma0
    alpha1 = gamma1 / (delta1 - beta * gamma1 / alpha0)
    for d in ARRIVAL:
        mult_ref[d] = alpha0 * z0[2 * d] + alpha1 * (z1[2 * d] + beta * z0[2 * d])
    for d in ARRIVAL:
        waits[4, 2 * d].wait_recv()
        image = own[3, 2 * d] + got[4, 2 * d] + beta * w0[2 * d]
        res_ref[d] = r1[2 * d] - alpha1 * image
    for copy in sent:
        copy.wait_send()


def shards(sizes, flexibility, stiffness, local_load, face_map, face_sign):
    order = flexibility.shape[-1]
    _, width, columns = local_load.shape[-3:]
    whole = (6, width, columns)
    half = (3, width, columns)
    dma = pltpu.SemaphoreType.DMA
    scratch = [
        pltpu.VMEM((2, order, order), jnp.bfloat16),
        pltpu.VMEM((order, order), jnp.bfloat16),
        pltpu.VMEM((2, order, order), jnp.bfloat16),
        pltpu.VMEM(whole, jnp.float32),
        pltpu.VMEM((4,) + whole, jnp.float32),
        pltpu.VMEM((5,) + whole, jnp.float32),
        pltpu.VMEM((order, columns), jnp.float32),
        pltpu.VMEM((5,) + whole, jnp.float32),
    ]
    scratch += [pltpu.VMEM((2, n, 2, 8, columns), jnp.float32) for n in sizes]
    scratch += [dma((3,)), dma((5, 6)), dma((5, 6))]
    for n in sizes:
        scratch += [dma((2, n)), dma((2, n))]
    any_space = pl.BlockSpec(memory_space=pl.ANY)
    vmem = pl.BlockSpec(memory_space=pltpu.VMEM)
    multipliers, residual = pl.pallas_call(
        functools.partial(kernel, sizes),
        out_shape=[jax.ShapeDtypeStruct(half, jnp.float32)] * 2,
        in_specs=[any_space, any_space, any_space, vmem, vmem],
        out_specs=[vmem, vmem],
        scratch_shapes=scratch,
        compiler_params=pltpu.CompilerParams(
            collective_id=0, has_side_effects=True, vmem_limit_bytes=60 * 1024 * 1024
        ),
        cost_estimate=pl.CostEstimate(
            flops=16 * order * order * columns, bytes_accessed=4 * order * order, transcendentals=0
        ),
    )(
        stiffness.reshape(order, order),
        flexibility.reshape(order, order),
        local_load.reshape(whole),
        face_map.reshape(6, width),
        face_sign.reshape(6, width),
    )
    return multipliers[None, None, None], residual[None, None, None]


def solution(mesh):
    sizes = tuple(mesh.shape[axis] for axis in AXES)
    matrix, face, line = (P(*AXES, *([None] * k)) for k in (2, 3, 2))
    return jax.shard_map(
        functools.partial(shards, sizes),
        mesh=mesh,
        in_specs=(matrix, matrix, face, line, line),
        out_specs=(face, face),
        check_vma=False,
    )
```

```python
import functools
import itertools
import math
import jax
import jax.numpy as jnp
from jax import lax
from jax.experimental import pallas as pl
from jax.experimental.pallas import tpu as pltpu
from jax.sharding import PartitionSpec as P

AXES = ("gx", "gy", "gz")
ARRIVAL = (1, 0, 2)
MESH = pl.DeviceIdType.MESH


def peers(sizes, me, group):
    found = []
    for offsets in itertools.product(*[range(sizes[d]) for d in group]):
        if any(offsets):
            where, slot = {}, 0
            for d, k in zip(group, offsets):
                index = lax.rem(me[d] + k, sizes[d]) if k else me[d]
                where[AXES[d]] = index
                slot = slot * sizes[d] + index
            found.append((where, slot))
    return found


def kernel(
    sizes, groups, stiff_hbm, flex_hbm, load_hbm, map_ref, sign_ref, mult_ref, res_ref,
    raw, mid, ops, load, own, got, acc, vec, local_sem, send_sem, recv_sem, *gathers
):
    width, columns = load.shape[1:]
    pair = 2 * width
    me = [lax.axis_index(axis) for axis in AXES]

    local = [
        pltpu.make_async_copy(load_hbm, load, local_sem.at[0]),
        pltpu.make_async_copy(stiff_hbm, raw.at[0], local_sem.at[1]),
        pltpu.make_async_copy(flex_hbm, raw.at[1], local_sem.at[2]),
    ]
    for copy in local:
        copy.start()

    barrier = pltpu.get_barrier_semaphore()
    others = [peer for group in groups for peer in peers(sizes, me, group)]
    for where, _ in others:
        pl.semaphore_signal(barrier, inc=1, device_id=where, device_id_type=MESH)
    pl.semaphore_wait(barrier, len(others))

    sent = []

    def send_face(exchange, face, source):
        d, upper = face // 2, face % 2
        step = 1 if upper else sizes[d] - 1
        there = face - 1 if upper else face + 1
        copy = pltpu.make_async_remote_copy(
            src_ref=source.at[face],
            dst_ref=got.at[exchange, there],
            send_sem=send_sem.at[exchange, face],
            recv_sem=recv_sem.at[exchange, there],
            device_id={AXES[d]: lax.rem(me[d] + step, sizes[d])},
            device_id_type=MESH,
        )
        copy.start()
        sent.append(copy)
        return copy

    def slot_of(group):
        index = 0
        for d in group:
            index = index * sizes[d] + me[d]
        return index

    def gather_start(which, stage, value):
        buf, ssem, rsem = gathers[3 * stage : 3 * stage + 3]
        mine = slot_of(groups[stage])
        buf[which, mine] = value
        for k, (where, _) in enumerate(peers(sizes, me, groups[stage])):
            copy = pltpu.make_async_remote_copy(
                src_ref=buf.at[which, mine],
                dst_ref=buf.at[which, mine],
                send_sem=ssem.at[which, k],
                recv_sem=rsem.at[which, mine],
                device_id=where,
                device_id_type=MESH,
            )
            copy.start()
            sent.append(copy)

    def gather_finish(which, stage):
        buf, ssem, rsem = gathers[3 * stage : 3 * stage + 3]
        for k, (where, slot) in enumerate(peers(sizes, me, groups[stage])):
            pltpu.make_async_remote_copy(
                src_ref=buf.at[which, slot],
                dst_ref=buf.at[which, slot],
                send_sem=ssem.at[which, k],
                recv_sem=rsem.at[which, slot],
                device_id=where,
                device_id_type=MESH,
            ).wait_recv()
        return jnp.sum(buf[which], axis=0)

    def rows(d):
        return slice(d * pair, (d + 1) * pair)

    def flat(value):
        return value.reshape(pair, columns)

    def faces(ref, d):
        return flat(ref[2 * d : 2 * d + 2])

    def fold(which):
        for d in range(3):
            low = map_ref[2 * d]
            high = map_ref[2 * d + 1] + width
            row = jnp.concatenate([low, high], axis=1)
            sign = jnp.concatenate(
                [sign_ref[2 * d], sign_ref[2 * d + 1]], axis=1
            ).astype(jnp.float32)
            place = lax.broadcasted_iota(jnp.int32, (pair, pair), 0)
            pick = jnp.where(place == row, sign, 0.0)
            mid[:, rows(d)] = jnp.dot(
                raw[which, :, rows(d)], pick.astype(jnp.bfloat16), preferred_element_type=jnp.float32
            ).astype(jnp.bfloat16)
        for d in range(3):
            low = map_ref[2 * d]
            high = map_ref[2 * d + 1] + width
            row = jnp.concatenate([low, high], axis=1)
            sign = jnp.concatenate(
                [sign_ref[2 * d], sign_ref[2 * d + 1]], axis=1
            ).astype(jnp.float32)
            place = lax.broadcasted_iota(jnp.int32, (pair, pair), 0)
            pick = jnp.where(place == row, sign, 0.0).T
            ops[which, rows(d), :] = jnp.dot(
                pick.astype(jnp.bfloat16), mid[rows(d), :], preferred_element_type=jnp.float32
            ).astype(jnp.bfloat16)

    def product(block, value, split):
        high = value.astype(jnp.bfloat16)
        if not split:
            return jnp.dot(block, high, preferred_element_type=jnp.float32)
        low = (value - high.astype(jnp.float32)).astype(jnp.bfloat16)
        both = jnp.dot(block, jnp.concatenate([high, low], axis=1), preferred_element_type=jnp.float32)
        return both[:, :columns] + both[:, columns:]

    def apply(which, get, out, split, ready=None):
        first = product(ops[which, :, rows(ARRIVAL[0])], get(ARRIVAL[0]), split)
        acc[...] = first
        acc[...] += product(ops[which, :, rows(ARRIVAL[1])], get(ARRIVAL[1]), split)
        last = get(ARRIVAL[2])
        for d in reversed(ARRIVAL):
            value = acc[rows(d), :] + product(ops[which, rows(d), rows(ARRIVAL[2])], last, split)
            own[out, 2 * d : 2 * d + 2] = value.reshape(2, width, columns)
            if ready is not None:
                ready(d)

    def sender(exchange):
        def ready(d):
            waits[exchange, 2 * d + 1] = send_face(exchange, 2 * d, own.at[exchange - 1])
            waits[exchange, 2 * d] = send_face(exchange, 2 * d + 1, own.at[exchange - 1])

        return ready

    waits = {}

    def arrive(exchange, d):
        waits[exchange, 2 * d].wait_recv()
        waits[exchange, 2 * d + 1].wait_recv()
        return flat(got[exchange, 2 * d : 2 * d + 2])

    def inner(first, second):
        total = jnp.zeros((8, columns), jnp.float32)
        for d in range(3):
            term = faces(first, d) * faces(second, d)
            total = total + jnp.sum(term.reshape(pair // 8, 8, columns), axis=0)
        return total

    def both(first, second):
        return jnp.concatenate(
            [jnp.sum(value, axis=0, keepdims=True) for value in (first, second)], axis=0
        )

    r0, z0, w0, r1, z1 = (vec.at[k] for k in range(5))

    def keep(ref, d, value):
        ref[2 * d : 2 * d + 2] = value.reshape(2, width, columns)
        return value

    for d in reversed(ARRIVAL):
        waits[0, 2 * d + 1] = send_face(0, 2 * d, load_hbm)
        waits[0, 2 * d] = send_face(0, 2 * d + 1, load_hbm)
    local[1].wait()
    fold(0)
    local[0].wait()
    apply(0, lambda d: keep(r0, d, faces(load, d) + arrive(0, d)), 0, True, sender(1))
    gamma_part = inner(r0, own.at[0])
    local[2].wait()
    fold(1)

    apply(1, lambda d: keep(z0, d, faces(own.at[0], d) + arrive(1, d)), 1, True)
    gather_start(0, 0, both(gamma_part, inner(z0, own.at[1])))
    for d in reversed(ARRIVAL):
        sender(2)(d)
    for stage in range(1, len(groups)):
        gather_start(0, stage, gather_finish(0, stage - 1))

    apply(0, lambda d: keep(w0, d, faces(own.at[1], d) + arrive(2, d)), 2, True, sender(3))
    sums = gather_finish(0, len(groups) - 1)
    gamma0, delta0 = sums[0:1], sums[1:2]
    alpha0 = gamma0 / delta0

    gamma_part = jnp.zeros((8, columns), jnp.float32)
    for d in range(3):
        value = keep(r1, d, faces(r0, d) - alpha0 * faces(w0, d))
        term = value * (faces(own.at[0], d) - alpha0 * faces(own.at[2], d))
        gamma_part = gamma_part + jnp.sum(term.reshape(pair // 8, 8, columns), axis=0)

    apply(
        1,
        lambda d: keep(z1, d, faces(z0, d) - alpha0 * (faces(own.at[2], d) + arrive(3, d))),
        3,
        True,
    )
    gather_start(1, 0, both(gamma_part, inner(z1, own.at[3])))
    for d in reversed(ARRIVAL):
        waits[4, 2 * d] = send_face(4, 2 * d + 1, own.at[3])
    for stage in range(1, len(groups)):
        gather_start(1, stage, gather_finish(1, stage - 1))
    sums = gather_finish(1, len(groups) - 1)
    gamma1, delta1 = sums[0:1], sums[1:2]
    beta = gamma1 / gamma0
    alpha1 = gamma1 / (delta1 - beta * gamma1 / alpha0)
    for d in ARRIVAL:
        mult_ref[d] = alpha0 * z0[2 * d] + alpha1 * (z1[2 * d] + beta * z0[2 * d])
    for d in ARRIVAL:
        waits[4, 2 * d].wait_recv()
        image = own[3, 2 * d] + got[4, 2 * d] + beta * w0[2 * d]
        res_ref[d] = r1[2 * d] - alpha1 * image
    for copy in sent:
        copy.wait_send()


def hand_over(mult_in, res_in, mult_out, res_out, sem):
    copies = [
        pltpu.make_async_copy(mult_in, mult_out, sem.at[0]),
        pltpu.make_async_copy(res_in, res_out, sem.at[1]),
    ]
    for copy in copies:
        copy.start()
    for copy in copies:
        copy.wait()


def shards(sizes, flexibility, stiffness, local_load, face_map, face_sign):
    order = flexibility.shape[-1]
    _, width, columns = local_load.shape[-3:]
    whole = (6, width, columns)
    half = (3, width, columns)
    dma = pltpu.SemaphoreType.DMA
    scratch = [
        pltpu.VMEM((2, order, order), jnp.bfloat16),
        pltpu.VMEM((order, order), jnp.bfloat16),
        pltpu.VMEM((2, order, order), jnp.bfloat16),
        pltpu.VMEM(whole, jnp.float32),
        pltpu.VMEM((4,) + whole, jnp.float32),
        pltpu.VMEM((5,) + whole, jnp.float32),
        pltpu.VMEM((order, columns), jnp.float32),
        pltpu.VMEM((5,) + whole, jnp.float32),
    ]
    scratch += [dma((3,)), dma((5, 6)), dma((5, 6))]
    groups = ((1, 0, 2),) if math.prod(sizes) <= 64 else ((1,), (0,), (2,))
    for group in groups:
        n = math.prod(sizes[d] for d in group)
        scratch += [pltpu.VMEM((2, n, 2, columns), jnp.float32), dma((2, n)), dma((2, n))]
    hbm = pl.BlockSpec(memory_space=pltpu.HBM)
    vmem = pl.BlockSpec(memory_space=pltpu.VMEM)
    multipliers, residual = pl.pallas_call(
        functools.partial(kernel, sizes, groups),
        out_shape=[jax.ShapeDtypeStruct(half, jnp.float32)] * 2,
        in_specs=[hbm, hbm, hbm, vmem, vmem],
        out_specs=[vmem, vmem],
        scratch_shapes=scratch,
        compiler_params=pltpu.CompilerParams(
            collective_id=0, has_side_effects=True, vmem_limit_bytes=60 * 1024 * 1024
        ),
        cost_estimate=pl.CostEstimate(
            flops=16 * order * order * columns, bytes_accessed=4 * order * order, transcendentals=0
        ),
    )(
        stiffness.reshape(order, order),
        flexibility.reshape(order, order),
        local_load.reshape(whole),
        face_map.reshape(6, 1, width),
        face_sign.reshape(6, 1, width),
    )
    multipliers, residual = pl.pallas_call(
        hand_over,
        out_shape=[jax.ShapeDtypeStruct(half, jnp.float32)] * 2,
        in_specs=[vmem, vmem],
        out_specs=[hbm, hbm],
        scratch_shapes=[dma((2,))],
    )(multipliers, residual)
    return multipliers[None, None, None], residual[None, None, None]


def solution(mesh):
    sizes = tuple(mesh.shape[axis] for axis in AXES)
    matrix, face, line = (P(*AXES, *([None] * k)) for k in (2, 3, 2))
    return jax.shard_map(
        functools.partial(shards, sizes),
        mesh=mesh,
        in_specs=(matrix, matrix, face, line, line),
        out_specs=(face, face),
        check_vma=False,
    )
```

```python
import functools
import itertools
import math
import jax
import jax.numpy as jnp
from jax import lax
from jax.experimental import pallas as pl
from jax.experimental.pallas import tpu as pltpu
from jax.sharding import PartitionSpec as P

AXES = ("gx", "gy", "gz")
ARRIVAL = (1, 0, 2)
MESH = pl.DeviceIdType.MESH


def peers(sizes, me, group):
    found = []
    for offsets in itertools.product(*[range(sizes[d]) for d in group]):
        if any(offsets):
            where, slot = {}, 0
            for d, k in zip(group, offsets):
                index = lax.rem(me[d] + k, sizes[d]) if k else me[d]
                where[AXES[d]] = index
                slot = slot * sizes[d] + index
            found.append((where, slot))
    return found


def kernel(
    sizes, groups, stiff_hbm, flex_hbm, load_hbm, map_ref, sign_ref, mult_ref, res_ref,
    raw, mid, ops, load, begin, own, got, acc, vec, local_sem, send_sem, recv_sem, *gathers
):
    width, columns = load.shape[1:]
    pair, short, lanes = 2 * width, width // 2, columns // 2
    me = [lax.axis_index(axis) for axis in AXES]

    local = [
        pltpu.make_async_copy(load_hbm, load, local_sem.at[0]),
        pltpu.make_async_copy(stiff_hbm, raw.at[0], local_sem.at[1]),
        pltpu.make_async_copy(flex_hbm, raw.at[1], local_sem.at[2]),
    ]
    for copy in local:
        copy.start()

    barrier = pltpu.get_barrier_semaphore()
    others = [peer for group in groups for peer in peers(sizes, me, group)]
    for where, _ in others:
        pl.semaphore_signal(barrier, inc=1, device_id=where, device_id_type=MESH)

    def turn(value):
        return pltpu.roll(value, lanes, 1)

    def merge(first, second):
        lane = lax.broadcasted_iota(jnp.int32, first.shape, 1)
        return jnp.where(lane < lanes, first, second)

    local[0].wait()
    for face in range(6):
        top, bottom = load[face, :short], load[face, short:]
        begin[0, face] = merge(top, turn(bottom))
        begin[1, face] = merge(turn(top), bottom)
    pl.semaphore_wait(barrier, len(others))

    sent = []
    waits = {}

    def send_face(half, exchange, face, source):
        d, upper = face // 2, face % 2
        step = 1 if upper else sizes[d] - 1
        there = face - 1 if upper else face + 1
        copy = pltpu.make_async_remote_copy(
            src_ref=source.at[face],
            dst_ref=got.at[half, exchange, there],
            send_sem=send_sem.at[half, exchange, face],
            recv_sem=recv_sem.at[half, exchange, there],
            device_id={AXES[d]: lax.rem(me[d] + step, sizes[d])},
            device_id_type=MESH,
        )
        copy.start()
        sent.append(copy)
        waits[half, exchange, there] = copy

    def slot_of(group):
        index = 0
        for d in group:
            index = index * sizes[d] + me[d]
        return index

    def gather_start(which, stage, value):
        buf, ssem, rsem = gathers[3 * stage : 3 * stage + 3]
        mine = slot_of(groups[stage])
        buf[which, mine] = value
        for k, (where, _) in enumerate(peers(sizes, me, groups[stage])):
            copy = pltpu.make_async_remote_copy(
                src_ref=buf.at[which, mine],
                dst_ref=buf.at[which, mine],
                send_sem=ssem.at[which, k],
                recv_sem=rsem.at[which, mine],
                device_id=where,
                device_id_type=MESH,
            )
            copy.start()
            sent.append(copy)

    def gather_finish(which, stage):
        buf, ssem, rsem = gathers[3 * stage : 3 * stage + 3]
        for k, (where, slot) in enumerate(peers(sizes, me, groups[stage])):
            pltpu.make_async_remote_copy(
                src_ref=buf.at[which, slot],
                dst_ref=buf.at[which, slot],
                send_sem=ssem.at[which, k],
                recv_sem=rsem.at[which, slot],
                device_id=where,
                device_id_type=MESH,
            ).wait_recv()
        return jnp.sum(buf[which], axis=0)

    def rows(d):
        return slice(d * pair, (d + 1) * pair)

    def faces(ref, d):
        return ref[2 * d : 2 * d + 2].reshape(width, columns)

    def keep(ref, d, value):
        ref[2 * d : 2 * d + 2] = value.reshape(2, short, columns)
        return value

    def picks(d):
        row = jnp.concatenate([map_ref[2 * d], map_ref[2 * d + 1] + width], axis=1)
        sign = jnp.concatenate([sign_ref[2 * d], sign_ref[2 * d + 1]], axis=1).astype(jnp.float32)
        place = lax.broadcasted_iota(jnp.int32, (pair, pair), 0)
        return jnp.where(place == row, sign, 0.0)

    def fold(which):
        for d in range(3):
            mid[:, rows(d)] = jnp.dot(
                raw[which, :, rows(d)],
                picks(d).astype(jnp.bfloat16),
                preferred_element_type=jnp.float32,
            ).astype(jnp.bfloat16)
        for d in range(3):
            ops[which, rows(d), :] = jnp.dot(
                picks(d).T.astype(jnp.bfloat16), mid[rows(d), :], preferred_element_type=jnp.float32
            ).astype(jnp.bfloat16)

    def spread(value):
        high = value.astype(jnp.bfloat16).astype(jnp.float32)
        low = value - high
        top, bottom = merge(high, turn(low)), merge(turn(high), low)
        return jnp.concatenate(
            [top[:short], bottom[:short], top[short:], bottom[short:]], axis=0
        ).astype(jnp.bfloat16)

    def dot(block, operand):
        return jnp.dot(block, operand, preferred_element_type=jnp.float32)

    def apply(which, get, out, ready=None):
        near, middle, far = ARRIVAL
        acc[...] = dot(ops[which, :, rows(near)], spread(get(near)))
        acc[...] += dot(ops[which, :, rows(middle)], spread(get(middle)))
        last = spread(get(far))
        for d in reversed(ARRIVAL):
            total = acc[rows(d), :] + dot(ops[which, rows(d), rows(far)], last)
            total = total + turn(total)
            out[2 * d] = merge(total[:short], total[short:width])
            out[2 * d + 1] = merge(total[width : width + short], total[width + short :])
            if ready is not None:
                ready(d)

    def sender(half, exchange, source):
        def ready(d):
            send_face(half, exchange, 2 * d, source)
            send_face(half, exchange, 2 * d + 1, source)

        return ready

    def arrive(half, exchange, d):
        waits[half, exchange, 2 * d].wait_recv()
        waits[half, exchange, 2 * d + 1].wait_recv()
        return faces(got.at[half, exchange], d)

    def fewer(term):
        return jnp.sum(term.reshape(width // 8, 8, columns), axis=0)

    def inner(first, second):
        return sum(fewer(faces(first, d) * faces(second, d)) for d in range(3))

    def message(parts):
        return jnp.concatenate(
            [jnp.sum(part + turn(part), axis=0, keepdims=True) for part in parts], axis=0
        )

    halves = range(2)
    v0, y0, u, y1 = ([own.at[h, k] for h in halves] for k in range(4))
    r0, z0, w0, r1, z1 = ([vec.at[h, k] for h in halves] for k in range(5))

    for h in halves:
        for d in reversed(ARRIVAL):
            sender(h, 0, begin.at[h])(d)
    local[1].wait()
    fold(0)

    for h in halves:
        apply(
            0,
            lambda d: keep(r0[h], d, faces(begin.at[h], d) + arrive(h, 0, d)),
            v0[h],
            sender(h, 1, v0[h]),
        )
    local[2].wait()
    fold(1)
    gamma_parts = [inner(r0[h], v0[h]) for h in halves]

    for h in halves:
        apply(
            1,
            lambda d: keep(z0[h], d, faces(v0[h], d) + arrive(h, 1, d)),
            y0[h],
            sender(h, 2, y0[h]),
        )
    gather_start(0, 0, message(gamma_parts + [inner(z0[h], y0[h]) for h in halves]))
    for stage in range(1, len(groups)):
        gather_start(0, stage, gather_finish(0, stage - 1))

    for h in halves:
        apply(
            0,
            lambda d: keep(w0[h], d, faces(y0[h], d) + arrive(h, 2, d)),
            u[h],
            sender(h, 3, u[h]),
        )
    sums = gather_finish(0, len(groups) - 1)
    gamma0, delta0 = sums[0:2], sums[2:4]
    alpha0 = gamma0 / delta0

    gamma_parts = []
    for h in halves:
        step = alpha0[h : h + 1]
        part = 0.0
        for d in range(3):
            value = keep(r1[h], d, faces(r0[h], d) - step * faces(w0[h], d))
            part = part + fewer(value * (faces(v0[h], d) - step * faces(u[h], d)))
        gamma_parts.append(part)

    def upper(half):
        def ready(d):
            send_face(half, 4, 2 * d + 1, y1[half])

        return ready

    for h in halves:
        apply(
            1,
            lambda d: keep(
                z1[h],
                d,
                faces(z0[h], d) - alpha0[h : h + 1] * (faces(u[h], d) + arrive(h, 3, d)),
            ),
            y1[h],
            None if h else upper(h),
        )
    gather_start(1, 0, message(gamma_parts + [inner(z1[h], y1[h]) for h in halves]))
    for d in reversed(ARRIVAL):
        upper(1)(d)
    for stage in range(1, len(groups)):
        gather_start(1, stage, gather_finish(1, stage - 1))
    sums = gather_finish(1, len(groups) - 1)
    gamma1, delta1 = sums[0:2], sums[2:4]
    beta = gamma1 / gamma0
    alpha1 = gamma1 / (delta1 - beta * gamma1 / alpha0)

    def put(ref, d, first, second):
        ref[d, :short] = merge(first, turn(second))
        ref[d, short:] = merge(turn(first), second)

    def scale(value, h):
        return value[h : h + 1]

    for d in ARRIVAL:
        put(mult_ref, d, *(
            scale(alpha0, h) * z0[h][2 * d]
            + scale(alpha1, h) * (z1[h][2 * d] + scale(beta, h) * z0[h][2 * d])
            for h in halves
        ))
    for d in ARRIVAL:
        for h in halves:
            waits[h, 4, 2 * d].wait_recv()
        put(res_ref, d, *(
            r1[h][2 * d]
            - scale(alpha1, h)
            * (y1[h][2 * d] + got[h, 4, 2 * d] + scale(beta, h) * w0[h][2 * d])
            for h in halves
        ))
    for copy in sent:
        copy.wait_send()


def hand_over(mult_in, res_in, mult_out, res_out, sem):
    copies = [
        pltpu.make_async_copy(mult_in, mult_out, sem.at[0]),
        pltpu.make_async_copy(res_in, res_out, sem.at[1]),
    ]
    for copy in copies:
        copy.start()
    for copy in copies:
        copy.wait()


def shards(sizes, flexibility, stiffness, local_load, face_map, face_sign):
    order = flexibility.shape[-1]
    _, width, columns = local_load.shape[-3:]
    whole = (6, width, columns)
    half = (3, width, columns)
    packed = (6, width // 2, columns)
    dma = pltpu.SemaphoreType.DMA
    scratch = [
        pltpu.VMEM((2, order, order), jnp.bfloat16),
        pltpu.VMEM((order, order), jnp.bfloat16),
        pltpu.VMEM((2, order, order), jnp.bfloat16),
        pltpu.VMEM(whole, jnp.float32),
        pltpu.VMEM((2,) + packed, jnp.float32),
        pltpu.VMEM((2, 4) + packed, jnp.float32),
        pltpu.VMEM((2, 5) + packed, jnp.float32),
        pltpu.VMEM((order, columns), jnp.float32),
        pltpu.VMEM((2, 5) + packed, jnp.float32),
    ]
    scratch += [dma((3,)), dma((2, 5, 6)), dma((2, 5, 6))]
    groups = ((1, 0, 2),) if math.prod(sizes) <= 64 else ((1,), (0,), (2,))
    for group in groups:
        n = math.prod(sizes[d] for d in group)
        scratch += [pltpu.VMEM((2, n, 4, columns), jnp.float32), dma((2, n)), dma((2, n))]
    hbm = pl.BlockSpec(memory_space=pltpu.HBM)
    vmem = pl.BlockSpec(memory_space=pltpu.VMEM)
    multipliers, residual = pl.pallas_call(
        functools.partial(kernel, sizes, groups),
        out_shape=[jax.ShapeDtypeStruct(half, jnp.float32)] * 2,
        in_specs=[hbm, hbm, hbm, vmem, vmem],
        out_specs=[vmem, vmem],
        scratch_shapes=scratch,
        compiler_params=pltpu.CompilerParams(
            collective_id=0, has_side_effects=True, vmem_limit_bytes=60 * 1024 * 1024
        ),
        cost_estimate=pl.CostEstimate(
            flops=16 * order * order * columns, bytes_accessed=4 * order * order, transcendentals=0
        ),
    )(
        stiffness.reshape(order, order),
        flexibility.reshape(order, order),
        local_load.reshape(whole),
        face_map.reshape(6, 1, width),
        face_sign.reshape(6, 1, width),
    )
    multipliers, residual = pl.pallas_call(
        hand_over,
        out_shape=[jax.ShapeDtypeStruct(half, jnp.float32)] * 2,
        in_specs=[vmem, vmem],
        out_specs=[hbm, hbm],
        scratch_shapes=[dma((2,))],
    )(multipliers, residual)
    return multipliers[None, None, None], residual[None, None, None]


def solution(mesh):
    sizes = tuple(mesh.shape[axis] for axis in AXES)
    matrix, face, line = (P(*AXES, *([None] * k)) for k in (2, 3, 2))
    return jax.shard_map(
        functools.partial(shards, sizes),
        mesh=mesh,
        in_specs=(matrix, matrix, face, line, line),
        out_specs=(face, face),
        check_vma=False,
    )
```

```python
import functools
import itertools
import math
import jax
import jax.numpy as jnp
from jax import lax
from jax.experimental import pallas as pl
from jax.experimental.pallas import tpu as pltpu
from jax.sharding import PartitionSpec as P

AXES = ("gx", "gy", "gz")
ARRIVAL = (1, 0, 2)
MESH = pl.DeviceIdType.MESH


def peers(sizes, me, group):
    found = []
    for offsets in itertools.product(*[range(sizes[d]) for d in group]):
        if any(offsets):
            where, slot = {}, 0
            for d, k in zip(group, offsets):
                index = lax.rem(me[d] + k, sizes[d]) if k else me[d]
                where[AXES[d]] = index
                slot = slot * sizes[d] + index
            found.append((where, slot))
    return found


def kernel(
    sizes, groups, stiff_hbm, flex_hbm, load_hbm, map_ref, sign_ref, mult_ref, res_ref,
    raw, mid, ops, load, own, got, acc, vec, local_sem, send_sem, recv_sem, *gathers
):
    width, columns = load.shape[1:]
    pair = 2 * width
    me = [lax.axis_index(axis) for axis in AXES]

    local = [
        pltpu.make_async_copy(load_hbm, load, local_sem.at[0]),
        pltpu.make_async_copy(stiff_hbm, raw.at[0], local_sem.at[1]),
        pltpu.make_async_copy(flex_hbm, raw.at[1], local_sem.at[2]),
    ]
    for copy in local:
        copy.start()

    barrier = pltpu.get_barrier_semaphore()
    others = [peer for group in groups for peer in peers(sizes, me, group)]
    for where, _ in others:
        pl.semaphore_signal(barrier, inc=1, device_id=where, device_id_type=MESH)
    pl.semaphore_wait(barrier, len(others))

    sent = []

    def send_face(exchange, face, source):
        d, upper = face // 2, face % 2
        step = 1 if upper else sizes[d] - 1
        there = face - 1 if upper else face + 1
        copy = pltpu.make_async_remote_copy(
            src_ref=source.at[face],
            dst_ref=got.at[exchange, there],
            send_sem=send_sem.at[exchange, face],
            recv_sem=recv_sem.at[exchange, there],
            device_id={AXES[d]: lax.rem(me[d] + step, sizes[d])},
            device_id_type=MESH,
        )
        copy.start()
        sent.append(copy)
        return copy

    def slot_of(group):
        index = 0
        for d in group:
            index = index * sizes[d] + me[d]
        return index

    def gather_start(which, stage, value):
        buf, ssem, rsem = gathers[3 * stage : 3 * stage + 3]
        mine = slot_of(groups[stage])
        buf[which, mine] = value
        for k, (where, _) in enumerate(peers(sizes, me, groups[stage])):
            copy = pltpu.make_async_remote_copy(
                src_ref=buf.at[which, mine],
                dst_ref=buf.at[which, mine],
                send_sem=ssem.at[which, k],
                recv_sem=rsem.at[which, mine],
                device_id=where,
                device_id_type=MESH,
            )
            copy.start()
            sent.append(copy)

    def gather_finish(which, stage):
        buf, ssem, rsem = gathers[3 * stage : 3 * stage + 3]
        for k, (where, slot) in enumerate(peers(sizes, me, groups[stage])):
            pltpu.make_async_remote_copy(
                src_ref=buf.at[which, slot],
                dst_ref=buf.at[which, slot],
                send_sem=ssem.at[which, k],
                recv_sem=rsem.at[which, slot],
                device_id=where,
                device_id_type=MESH,
            ).wait_recv()
        return jnp.sum(buf[which], axis=0)

    def rows(d):
        return slice(d * pair, (d + 1) * pair)

    def flat(value):
        return value.reshape(pair, columns)

    def faces(ref, d):
        return flat(ref[2 * d : 2 * d + 2])

    def fold(which):
        for d in range(3):
            low = map_ref[2 * d]
            high = map_ref[2 * d + 1] + width
            row = jnp.concatenate([low, high], axis=1)
            sign = jnp.concatenate(
                [sign_ref[2 * d], sign_ref[2 * d + 1]], axis=1
            ).astype(jnp.float32)
            place = lax.broadcasted_iota(jnp.int32, (pair, pair), 0)
            pick = jnp.where(place == row, sign, 0.0)
            mid[:, rows(d)] = jnp.dot(
                raw[which, :, rows(d)], pick.astype(jnp.bfloat16), preferred_element_type=jnp.float32
            ).astype(jnp.bfloat16)
        for d in range(3):
            low = map_ref[2 * d]
            high = map_ref[2 * d + 1] + width
            row = jnp.concatenate([low, high], axis=1)
            sign = jnp.concatenate(
                [sign_ref[2 * d], sign_ref[2 * d + 1]], axis=1
            ).astype(jnp.float32)
            place = lax.broadcasted_iota(jnp.int32, (pair, pair), 0)
            pick = jnp.where(place == row, sign, 0.0).T
            ops[which, rows(d), :] = jnp.dot(
                pick.astype(jnp.bfloat16), mid[rows(d), :], preferred_element_type=jnp.float32
            ).astype(jnp.bfloat16)

    def product(block, value, split):
        high = value.astype(jnp.bfloat16)
        if not split:
            return jnp.dot(block, high, preferred_element_type=jnp.float32)
        low = (value - high.astype(jnp.float32)).astype(jnp.bfloat16)
        both = jnp.dot(block, jnp.concatenate([high, low], axis=1), preferred_element_type=jnp.float32)
        return both[:, :columns] + both[:, columns:]

    def apply(which, get, out, split, ready=None):
        first = product(ops[which, :, rows(ARRIVAL[0])], get(ARRIVAL[0]), split)
        acc[...] = first
        acc[...] += product(ops[which, :, rows(ARRIVAL[1])], get(ARRIVAL[1]), split)
        last = get(ARRIVAL[2])
        for d in reversed(ARRIVAL):
            value = acc[rows(d), :] + product(ops[which, rows(d), rows(ARRIVAL[2])], last, split)
            own[out, 2 * d : 2 * d + 2] = value.reshape(2, width, columns)
            if ready is not None:
                ready(d)

    def sender(exchange):
        def ready(d):
            waits[exchange, 2 * d + 1] = send_face(exchange, 2 * d, own.at[exchange - 1])
            waits[exchange, 2 * d] = send_face(exchange, 2 * d + 1, own.at[exchange - 1])

        return ready

    waits = {}

    def arrive(exchange, d):
        waits[exchange, 2 * d].wait_recv()
        waits[exchange, 2 * d + 1].wait_recv()
        return flat(got[exchange, 2 * d : 2 * d + 2])

    def inner(first, second):
        total = jnp.zeros((8, columns), jnp.float32)
        for d in range(3):
            term = faces(first, d) * faces(second, d)
            total = total + jnp.sum(term.reshape(pair // 8, 8, columns), axis=0)
        return total

    def both(first, second):
        return jnp.concatenate(
            [jnp.sum(value, axis=0, keepdims=True) for value in (first, second)], axis=0
        )

    r0, z0, w0, r1, z1 = (vec.at[k] for k in range(5))

    def keep(ref, d, value):
        ref[2 * d : 2 * d + 2] = value.reshape(2, width, columns)
        return value

    for d in reversed(ARRIVAL):
        waits[0, 2 * d + 1] = send_face(0, 2 * d, load_hbm)
        waits[0, 2 * d] = send_face(0, 2 * d + 1, load_hbm)
    local[1].wait()
    fold(0)
    local[0].wait()
    apply(0, lambda d: keep(r0, d, faces(load, d) + arrive(0, d)), 0, True, sender(1))
    gamma_part = inner(r0, own.at[0])
    local[2].wait()
    fold(1)

    apply(1, lambda d: keep(z0, d, faces(own.at[0], d) + arrive(1, d)), 1, True)
    gather_start(0, 0, both(gamma_part, inner(z0, own.at[1])))
    for d in reversed(ARRIVAL):
        sender(2)(d)
    for stage in range(1, len(groups)):
        gather_start(0, stage, gather_finish(0, stage - 1))

    apply(0, lambda d: keep(w0, d, faces(own.at[1], d) + arrive(2, d)), 2, True, sender(3))
    sums = gather_finish(0, len(groups) - 1)
    gamma0, delta0 = sums[0:1], sums[1:2]
    alpha0 = gamma0 / delta0

    gamma_part = jnp.zeros((8, columns), jnp.float32)
    for d in range(3):
        value = keep(r1, d, faces(r0, d) - alpha0 * faces(w0, d))
        term = value * (faces(own.at[0], d) - alpha0 * faces(own.at[2], d))
        gamma_part = gamma_part + jnp.sum(term.reshape(pair // 8, 8, columns), axis=0)

    apply(
        1,
        lambda d: keep(z1, d, faces(z0, d) - alpha0 * (faces(own.at[2], d) + arrive(3, d))),
        3,
        True,
    )
    gather_start(1, 0, both(gamma_part, inner(z1, own.at[3])))
    for d in reversed(ARRIVAL):
        waits[4, 2 * d] = send_face(4, 2 * d + 1, own.at[3])
    for stage in range(1, len(groups)):
        gather_start(1, stage, gather_finish(1, stage - 1))
    sums = gather_finish(1, len(groups) - 1)
    gamma1, delta1 = sums[0:1], sums[1:2]
    beta = gamma1 / gamma0
    alpha1 = gamma1 / (delta1 - beta * gamma1 / alpha0)
    for d in ARRIVAL:
        mult_ref[d] = alpha0 * z0[2 * d] + alpha1 * (z1[2 * d] + beta * z0[2 * d])
    for d in ARRIVAL:
        waits[4, 2 * d].wait_recv()
        image = own[3, 2 * d] + got[4, 2 * d] + beta * w0[2 * d]
        res_ref[d] = r1[2 * d] - alpha1 * image
    for copy in sent:
        copy.wait_send()


def shards(sizes, flexibility, stiffness, local_load, face_map, face_sign):
    order = flexibility.shape[-1]
    _, width, columns = local_load.shape[-3:]
    whole = (6, width, columns)
    half = (3, width, columns)
    dma = pltpu.SemaphoreType.DMA
    scratch = [
        pltpu.VMEM((2, order, order), jnp.bfloat16),
        pltpu.VMEM((order, order), jnp.bfloat16),
        pltpu.VMEM((2, order, order), jnp.bfloat16),
        pltpu.VMEM(whole, jnp.float32),
        pltpu.VMEM((4,) + whole, jnp.float32),
        pltpu.VMEM((5,) + whole, jnp.float32),
        pltpu.VMEM((order, columns), jnp.float32),
        pltpu.VMEM((5,) + whole, jnp.float32),
    ]
    scratch += [dma((3,)), dma((5, 6)), dma((5, 6))]
    groups = ((1, 0, 2),) if math.prod(sizes) <= 64 else ((1,), (0,), (2,))
    for group in groups:
        n = math.prod(sizes[d] for d in group)
        scratch += [pltpu.VMEM((2, n, 2, columns), jnp.float32), dma((2, n)), dma((2, n))]
    hbm = pl.BlockSpec(memory_space=pltpu.HBM)
    vmem = pl.BlockSpec(memory_space=pltpu.VMEM)
    multipliers, residual = pl.pallas_call(
        functools.partial(kernel, sizes, groups),
        out_shape=[pltpu.VMEM(half, jnp.float32)] * 2,
        in_specs=[hbm, hbm, hbm, vmem, vmem],
        out_specs=[vmem, vmem],
        scratch_shapes=scratch,
        compiler_params=pltpu.CompilerParams(
            collective_id=0, has_side_effects=True, vmem_limit_bytes=60 * 1024 * 1024
        ),
        cost_estimate=pl.CostEstimate(
            flops=16 * order * order * columns, bytes_accessed=4 * order * order, transcendentals=0
        ),
    )(
        stiffness.reshape(order, order),
        flexibility.reshape(order, order),
        local_load.reshape(whole),
        face_map.reshape(6, 1, width),
        face_sign.reshape(6, 1, width),
    )
    return multipliers[None, None, None], residual[None, None, None]


def solution(mesh):
    sizes = tuple(mesh.shape[axis] for axis in AXES)
    matrix, face, line = (P(*AXES, *([None] * k)) for k in (2, 3, 2))
    return jax.shard_map(
        functools.partial(shards, sizes),
        mesh=mesh,
        in_specs=(matrix, matrix, face, line, line),
        out_specs=(face, face),
        check_vma=False,
    )
```
